32 devices in a mesh: chain: 8 (over z, y), spatial: 2 (over x), dp: 2 (over core).
Axes of the slice: x: 2, y: 2, z: 4, core: 2. Of those that a mesh axis runs over, the one named last changes fastest.
Arguments:
- images: bfloat16 [4, 2, 16, 16, 512], P(None, 'dp', 'spatial'), may hold values from -6 to 6
- cotangent: bfloat16 [4, 2, 16, 16, 512], P(None, 'dp', 'spatial'), may hold values from -0.3125 to 0.3125
- weights: bfloat16 [8, 9, 512, 512], P('chain'), may hold values from -0.046875 to 0.046875
Outputs:
- weight_grads: float32 [8, 9, 512, 512], P('chain', None, ('spatial', 'dp'))
The draws below stay inside these ranges and needn't reach their ends.
All inputs are finite; a program needn't handle non-finite values.
Results may differ from the reference program's by a relative error of at most 0.015.
Values may be sent and summed in bfloat16 or wider, within the bound.
A program may use at most 64 MiB of HBM per device.

```python
import jax
import jax.numpy as jnp
from jax import lax

C = 512
MB = 4
WW = 16
SECTIONS = 8
BATCH = 2
H = 16


def level_of(rng, extent, pieces, least, top_value):
    level = 1.0
    for position, blocks in pieces:
        steps = jax.random.uniform(jax.random.fold_in(jax.random.fold_in(rng, 6), position), (blocks,), jnp.float32, least / len(pieces), top_value / len(pieces))
        level = level * jnp.repeat(jnp.exp(steps), extent[position] // blocks).reshape((-1,) + (1,) * (len(extent) - 1 - position))
    return level


def centred(rng, extent, width, bound, cuts=(), held_as=jnp.bfloat16):
    factor_of = level_of(rng, extent, cuts, -0.22, 0.18) if cuts else 1.0
    array = jax.random.normal(rng, extent, jnp.float32) * width * factor_of
    return jnp.minimum(jnp.maximum(array, -bound), bound).astype(held_as)


def setup_inputs(seed: int = 0) -> dict:
    key_of = jax.random.split(jax.random.key(seed), 4)
    images = centred(key_of[0], (MB, BATCH, H, WW, C), 1.0, 6.0, ((1, 2), (2, 2)))
    cotangent = centred(key_of[1], (MB, BATCH, H, WW, C), ((MB * BATCH * H * WW) ** -0.5), 0.3125, ((1, 2), (2, 2)))
    weights = centred(key_of[2], (SECTIONS, 9, C, C), (36 * C) ** -0.5, 0.046875, ((0, 8),))
    return dict(images=images, cotangent=cotangent, weights=weights)


def patches(padded, rows, cols, reverse):
    offsets = [(a, b) for a in range(3) for b in range(3)]
    if reverse:
        offsets = offsets[::-1]
    parts = [padded[:, a:a + rows, b:b + cols, :] for a, b in offsets]
    return jnp.stack(parts, axis=-2).reshape(-1, 9, padded.shape[-1])


def pad_map(field):
    return jnp.pad(field, ((0, 0), (1, 1), (1, 1), (0, 0)))


def silu_slope(value):
    sig = jax.nn.sigmoid(value)
    return sig * (1.0 + value * (1.0 - sig))


def reference(images, cotangent, weights):
    field = images.reshape(MB * BATCH, H, WW, C)
    inputs = []
    states = []
    for section in range(SECTIONS):
        inputs.append(field)
        cols = patches(pad_map(field), H, WW, False).reshape(-1, 9 * C)
        state = jnp.dot(cols, weights[section].reshape(9 * C, C), preferred_element_type=jnp.float32)
        states.append(state)
        field = (field.astype(jnp.float32) + jax.nn.silu(state).reshape(field.shape)).astype(jnp.bfloat16)
    upstream = cotangent.reshape(MB * BATCH, H, WW, C)
    grads = []
    for section in range(SECTIONS - 1, -1, -1):
        delta = (upstream.astype(jnp.float32).reshape(-1, C) * silu_slope(states[section])).astype(jnp.bfloat16)
        cols = patches(pad_map(inputs[section]), H, WW, False).reshape(-1, 9 * C)
        grad = lax.dot_general(cols, delta, (((0,), (0,)), ((), ())), preferred_element_type=jnp.float32)
        grads.append(grad.reshape(9, C, C))
        if section > 0:
            back = patches(pad_map(delta.reshape(upstream.shape)), H, WW, True)
            flow = jnp.einsum("nkc,kdc->nd", back, weights[section], preferred_element_type=jnp.float32)
            upstream = (upstream.astype(jnp.float32) + flow.reshape(upstream.shape)).astype(jnp.bfloat16)
    return jnp.stack(grads[::-1], axis=0)
```

```python
import jax
import jax.numpy as jnp
from jax import lax
from jax.experimental import pallas as pl
from jax.experimental.pallas import tpu as pltpu
from jax.sharding import PartitionSpec as P


def with_halo(cells, sides, width):
    for axis, dim in sides:
        count = lax.axis_size(axis)
        ends = count - 1
        head = lax.slice_in_dim(cells, 0, width, axis=dim)
        tail = lax.slice_in_dim(cells, cells.shape[dim] - width, cells.shape[dim], axis=dim)
        cells = jnp.concatenate(
            [
                lax.ppermute(tail, axis, [(i, (i + 1) % count) for i in range(ends)]),
                cells,
                lax.ppermute(head, axis, [((i + 1) % count, i) for i in range(ends)]),
            ],
            axis=dim,
        )
    return cells


def passed_along(block, axis, distance):
    devices = range(lax.axis_size(axis))
    route = [(i - distance, i) for i in devices if i - distance in devices]
    return lax.ppermute(block, axis, route)


def patches(padded, rows, cols, reverse):
    offsets = [(a, b) for a in range(3) for b in range(3)]
    if reverse:
        offsets = offsets[::-1]
    parts = [padded[:, a : a + rows, b : b + cols, :] for a, b in offsets]
    return jnp.stack(parts, axis=-2).reshape(-1, 9, padded.shape[-1])


def pad_cols(field):
    return jnp.pad(field, ((0, 0), (0, 0), (1, 1), (0, 0)))


def silu_slope(value):
    sig = jax.nn.sigmoid(value)
    return sig * (1.0 + value * (1.0 - sig))


def shards(images, cotangent, weights):
    micros, imgs, height, width, chans = images.shape
    pixels = imgs * height * width
    sections = lax.axis_size("chain")
    section = lax.axis_index("chain")
    ticks = micros + sections - 1
    kernel = weights[0]
    flat_kernel = kernel.reshape(9 * chans, chans)
    shape_one = (imgs, height, width, chans)

    def forward_tick(tick, carry):
        inbox, saved_x, saved_z = carry
        micro = tick - section
        valid = jnp.logical_and(micro >= 0, micro < micros)
        slot = jnp.clip(micro, 0, micros - 1)
        first = lax.dynamic_index_in_dim(images, slot, 0, keepdims=False)
        source = jnp.where(section == 0, first, inbox)
        rows = with_halo(source, (("spatial", 1),), 1)
        padded = pad_cols(rows)

        def forward_active(operand):
            cols = patches(operand, height, width, False).reshape(-1, 9 * chans)
            state = jnp.dot(cols, flat_kernel, preferred_element_type=jnp.float32)
            output = (source.astype(jnp.float32) + jax.nn.silu(state).reshape(shape_one)).astype(
                jnp.bfloat16
            )
            return (output, state)

        def forward_resting(operand):
            return (jnp.zeros(shape_one, jnp.bfloat16), jnp.zeros((pixels, chans), jnp.float32))

        output, state = lax.cond(valid, forward_active, forward_resting, padded)
        saved_x = jnp.where(
            valid, lax.dynamic_update_index_in_dim(saved_x, padded, slot, 0), saved_x
        )
        saved_z = jnp.where(
            valid, lax.dynamic_update_index_in_dim(saved_z, state, slot, 0), saved_z
        )
        inbox = passed_along(output, "chain", 1)
        return (inbox, saved_x, saved_z)

    start = (
        jnp.zeros(shape_one, jnp.bfloat16),
        jnp.zeros((micros, imgs, height + 2, width + 2, chans), jnp.bfloat16),
        jnp.zeros((micros, pixels, chans), jnp.float32),
    )
    inbox, saved_x, saved_z = lax.fori_loop(0, ticks, forward_tick, start)

    def backward_tick(tick, carry):
        inbox, saved_d = carry
        micro = tick - (sections - 1 - section)
        valid = jnp.logical_and(micro >= 0, micro < micros)
        slot = jnp.clip(micro, 0, micros - 1)
        last = lax.dynamic_index_in_dim(cotangent, slot, 0, keepdims=False)
        upstream = jnp.where(section == sections - 1, last, inbox)
        state = lax.dynamic_index_in_dim(saved_z, slot, 0, keepdims=False)
        delta = (upstream.astype(jnp.float32).reshape(pixels, chans) * silu_slope(state)).astype(
            jnp.bfloat16
        )
        delta = jnp.where(valid, delta, jnp.zeros_like(delta))
        rows = with_halo(delta.reshape(shape_one), (("spatial", 1),), 1)
        padded = pad_cols(rows)

        def backward_active(operand):
            back = patches(operand, height, width, True)
            flow = jnp.einsum("nkc,kdc->nd", back, kernel, preferred_element_type=jnp.float32)
            return (upstream.astype(jnp.float32) + flow.reshape(shape_one)).astype(jnp.bfloat16)

        def backward_resting(operand):
            return jnp.zeros(shape_one, jnp.bfloat16)

        result = lax.cond(valid, backward_active, backward_resting, padded)
        saved_d = jnp.where(
            valid, lax.dynamic_update_index_in_dim(saved_d, delta, slot, 0), saved_d
        )
        inbox = passed_along(result, "chain", -1)
        return (inbox, saved_d)

    begin = (jnp.zeros(shape_one, jnp.bfloat16), jnp.zeros((micros, pixels, chans), jnp.bfloat16))
    inbox, saved_d = lax.fori_loop(0, ticks, backward_tick, begin)
    cols_all = patches(
        saved_x.reshape(micros * imgs, height + 2, width + 2, chans), height, width, False
    )
    cols_all = cols_all.reshape(-1, 9 * chans)
    local_grad = lax.dot_general(
        cols_all,
        saved_d.reshape(-1, chans),
        (((0,), (0,)), ((), ())),
        preferred_element_type=jnp.float32,
    ).reshape(9, chans, chans)
    summed = lax.psum_scatter(
        local_grad.astype(jnp.bfloat16), ("spatial", "dp"), scatter_dimension=1, tiled=True
    ).astype(jnp.float32)
    return summed[None]

LANES = 128
MESH = pl.DeviceIdType.MESH


def pipeline_kernel(
    images, cotangent, weights, out,
    w, wt, xin, xout, gin, gout, slope, dall, xs, xt, acc, cat, grad,
    w_sem, loc_sem, out_sem,
    f_send, x_send, x_recv, xh_send, xh_recv,
    g_send, g_recv, gh_send, gh_recv,
    s_send, s_recv, xs_send, xs_recv, d_send, d_recv,
):
    micros, quarters, padded_rows, cols, _ = xin.shape
    rows = padded_rows - 2
    pixels = rows * cols
    chans = quarters * LANES
    half = chans // 2
    hq = quarters // 2
    stage = lax.axis_index("chain")
    last = lax.axis_size("chain") - 1
    sp = lax.axis_index("spatial")
    dp = lax.axis_index("dp")
    osp, odp = 1 - sp, 1 - dp
    me = sp * 2 + dp
    mates = ((sp, odp), (osp, dp), (osp, odp))
    edge_src = (rows - 1) * osp
    edge_dst = (rows + 1) * sp

    def remote(src, dst, send, recv, chain, spatial, core):
        return pltpu.make_async_remote_copy(
            src_ref=src, dst_ref=dst, send_sem=send, recv_sem=recv,
            device_id=(chain, spatial, core), device_id_type=MESH,
        )

    def x_main(m, c):
        return remote(
            xout.at[m, pl.ds(c * hq, hq)], xin.at[m, pl.ds(c * hq, hq), pl.ds(1, rows)],
            x_send.at[m, c], x_recv.at[m, c], stage + 1, sp, dp)

    def x_edge(m, c):
        return remote(
            xout.at[m, pl.ds(c * hq, hq), pl.ds(edge_src, 1)],
            xin.at[m, pl.ds(c * hq, hq), pl.ds(edge_dst, 1)],
            xh_send.at[m, c], xh_recv.at[m, c], stage + 1, osp, dp)

    def x_first(m, c):
        return remote(
            xin.at[m, pl.ds(c * hq, hq), pl.ds(1 + edge_src, 1)],
            xin.at[m, pl.ds(c * hq, hq), pl.ds(edge_dst, 1)],
            f_send.at[m, c], xh_recv.at[m, c], stage, osp, dp)

    def g_main(m, c):
        return remote(
            gout.at[m, pl.ds(c * hq, hq)], gin.at[m, pl.ds(c * hq, hq), pl.ds(1, rows)],
            g_send.at[m, c], g_recv.at[m, c], stage - 1, sp, dp)

    def g_edge(m, c):
        return remote(
            gout.at[m, pl.ds(c * hq, hq), pl.ds(edge_src, 1)],
            gin.at[m, pl.ds(c * hq, hq), pl.ds(edge_dst, 1)],
            gh_send.at[m, c], gh_recv.at[m, c], stage - 1, osp, dp)

    def g_first(m, c):
        return remote(
            gin.at[m, pl.ds(c * hq, hq), pl.ds(1 + edge_src, 1)],
            gin.at[m, pl.ds(c * hq, hq), pl.ds(edge_dst, 1)],
            f_send.at[m, c], gh_recv.at[m, c], stage, osp, dp)

    def slope_edge(m):
        return remote(
            slope.at[m, :, pl.ds(1 + edge_src, 1)], slope.at[m, :, pl.ds(edge_dst, 1)],
            s_send.at[m], s_recv.at[m], stage, osp, dp)

    def x_slice(m, j):
        a, b = mates[j]
        return remote(
            xin.at[m, a * 2 + b, pl.ds(1, rows)], xs.at[m, me],
            xs_send.at[m, j], xs_recv.at[m, j], stage, a, b)

    def d_block(m, c, j):
        a, b = ((sp, odp), (osp, dp), (sp, odp))[j]
        owner = me if j < 2 else osp * 2 + dp
        block = dall.at[m, owner, pl.ds(c * hq, hq)]
        return remote(block, block, d_send.at[m, j, c], d_recv.at[m, j, c], stage, a, b)

    def local_in(array, buffer, m, q):
        return pltpu.make_async_copy(
            array.at[m, :, :, pl.ds(q * LANES, LANES)], buffer.at[m, q, pl.ds(1, rows)],
            loc_sem.at[m, q])

    w_copy = pltpu.make_async_copy(weights, w, w_sem)
    w_copy.start()

    @pl.when(stage == 0)
    def _():
        for m in range(micros):
            for q in range(quarters):
                local_in(images, xin, m, q).start()

    @pl.when(stage == last)
    def _():
        for m in range(micros):
            for q in range(quarters):
                local_in(cotangent, gin, m, q).start()

    barrier = pltpu.get_barrier_semaphore()

    def greet(chain, spatial, core):
        pl.semaphore_signal(barrier, inc=1, device_id=(chain, spatial, core), device_id_type=MESH)

    for a, b in mates:
        greet(stage, a, b)

    @pl.when(stage > 0)
    def _():
        greet(stage - 1, sp, dp)
        greet(stage - 1, osp, dp)

    @pl.when(stage < last)
    def _():
        greet(stage + 1, sp, dp)
        greet(stage + 1, osp, dp)

    zero_row = (rows + 1) * sp
    blank = jnp.zeros((micros, quarters, 1, cols, LANES), jnp.float32)
    xin[:, :, pl.ds(zero_row, 1)] = blank.astype(xin.dtype)
    gin[:, :, pl.ds(zero_row, 1)] = blank.astype(gin.dtype)
    slope[:, :, pl.ds(zero_row, 1)] = blank
    grad[...] = jnp.zeros_like(grad)

    around = jnp.where(stage > 0, 2, 0) + jnp.where(stage < last, 2, 0)
    pl.semaphore_wait(barrier, 3 + around)

    @pl.when(stage == 0)
    def _():
        for m in range(micros):
            for q in range(quarters):
                local_in(images, xin, m, q).wait()
            for c in range(2):
                x_first(m, c).start()

    @pl.when(stage == last)
    def _():
        for m in range(micros):
            for q in range(quarters):
                local_in(cotangent, gin, m, q).wait()
            for c in range(2):
                g_first(m, c).start()

    w_copy.wait()

    @pl.when(stage > 0)
    def _():
        @pl.loop(0, 9)
        def _(k):
            wt[k] = w[8 - k].T

    def column_shifts(value):
        n = value.shape[0]
        col = lax.broadcasted_iota(jnp.int32, value.shape, 0) % cols
        before = jnp.where(col == 0, 0.0, pltpu.roll(value, 1, 0))
        after = jnp.where(col == cols - 1, 0.0, pltpu.roll(value, n - 1, 0))
        return before, value, after

    def load_half(ref, m, c):
        parts = [ref[m, c * hq + i].astype(jnp.float32) for i in range(hq)]
        return jnp.concatenate(parts, axis=-1)

    def spread(value, c):
        shifted = column_shifts(value.reshape(padded_rows * cols, half))
        joined = jnp.concatenate([v.astype(cat.dtype) for v in shifted], axis=-1)
        cat[c] = joined.reshape(padded_rows, cols, 3 * half)

    def product(kernel, c, lo, width):
        lhs = jnp.concatenate(
            [cat[c, pl.ds(a, rows)].reshape(pixels, 3 * half) for a in range(3)], axis=-1)
        rhs = kernel[:, pl.ds(c * half, half), pl.ds(lo, width)].reshape(9 * half, width)
        return jnp.dot(lhs, rhs, preferred_element_type=jnp.float32)

    def store_half(ref, m, n, first, value):
        for i in range(hq):
            part = value[:, i * LANES:(i + 1) * LANES].reshape(rows, cols, LANES)
            ref[m, n * hq + i, pl.ds(first, rows)] = part.astype(ref.dtype)

    def forward(m):
        for c in range(2):
            @pl.when(stage > 0)
            def _():
                x_main(m, c).wait_recv()

            x_edge(m, c).wait_recv()
            spread(load_half(xin, m, c), c)
            if c == 0:
                acc[...] = product(w, 0, 0, chans)
        for n in range(2):
            z = acc[:, pl.ds(n * half, half)] + product(w, 1, n * half, half)
            sig = jax.nn.sigmoid(z)
            own = load_half(xin, m, n)[1:rows + 1].reshape(pixels, half)
            store_half(xout, m, n, 0, own + z * sig)

            @pl.when(stage < last)
            def _():
                x_main(m, n).start()
                x_edge(m, n).start()

            store_half(slope, m, n, 1, sig * (1.0 + z * (1.0 - sig)))
        slope_edge(m).start()
        for j in range(3):
            x_slice(m, j).start()
        xs[m, me] = xin[m, me, pl.ds(1, rows)]

    def backward(m):
        slope_edge(m).wait_recv()
        for c in range(2):
            @pl.when(stage < last)
            def _():
                g_main(m, c).wait_recv()

            g_edge(m, c).wait_recv()

            d = (load_half(gin, m, c) * load_half(slope, m, c)).astype(dall.dtype)
            for i in range(hq):
                dall[m, me, c * hq + i] = d[1:rows + 1, :, i * LANES:(i + 1) * LANES].reshape(
                    pixels, LANES)
            @pl.when(stage > 0)
            def _():
                spread(d.astype(jnp.float32), c)
                if c == 0:
                    acc[...] = product(wt, 0, 0, chans)

            d_block(m, c, 1).start()
            d_block(m, c, 0).start()

        @pl.when(stage > 0)
        def _():
            for n in range(2):
                own = load_half(gin, m, n)[1:rows + 1].reshape(pixels, half)
                flow = acc[:, pl.ds(n * half, half)] + product(wt, 1, n * half, half)
                store_half(gout, m, n, 0, own + flow)
                g_main(m, n).start()
                g_edge(m, n).start()

    def prepare(m):
        for j in range(3):
            x_slice(m, j).wait_recv()
        for image in range(2):
            tall = jnp.concatenate([xs[m, image], xs[m, 2 + image]], axis=0).astype(jnp.float32)
            blank_row = jnp.zeros((1, cols, LANES), jnp.float32)
            shifted = column_shifts(tall.reshape(2 * pixels, LANES))
            for b in range(3):
                field = jnp.concatenate(
                    [blank_row, shifted[b].reshape(2 * rows, cols, LANES), blank_row], axis=0)
                for part in range(2):
                    for a in range(3):
                        lo = part * rows + a
                        block = field[lo:lo + rows].reshape(pixels, LANES)
                        xt[m, part, 3 * a + b, :, pl.ds(image * LANES, LANES)] = block.T.astype(
                            xt.dtype)

    def add_grad(m, part):
        blocks = []
        for image in range(2):
            blocks.append(jnp.concatenate(
                [dall[m, part * 2 + image, q] for q in range(quarters)], axis=-1))
        rhs = jnp.concatenate(blocks, axis=0)
        for a in range(3):
            lhs = xt[m, part, pl.ds(3 * a, 3)].reshape(3 * LANES, 2 * pixels)
            total = jnp.dot(lhs, rhs, preferred_element_type=jnp.float32)
            grad[pl.ds(3 * a, 3)] += total.reshape(3, LANES, chans)

    def accumulate(m):
        for c in range(2):
            d_block(m, c, 0).wait_recv()
        add_grad(m, sp)
        for c in range(2):
            d_block(m, c, 1).wait_recv()
            d_block(m, c, 2).start()
        for c in range(2):
            d_block(m, c, 2).wait_recv()
        add_grad(m, osp)

    F, B, Q, W = ([k * micros + i for i in range(micros)] for k in range(4))
    early = F + Q + [B[0]]
    for i in range(1, micros):
        early += [B[i], W[i - 1]]
    early += [W[-1]]
    late = F + B + Q + W
    final = [v for pair in zip(F, B) for v in pair] + Q + W

    @pl.loop(0, 4 * micros)
    def _(step):
        code = jnp.int32(0)
        for i in range(4 * micros):
            choice = jnp.where(
                stage == last, final[i], jnp.where(stage * 2 < last + 1, early[i], late[i]))
            code = jnp.where(step == i, choice, code)
        kind = code // micros
        m = code % micros

        @pl.when(kind == 0)
        def _():
            forward(m)

        @pl.when(kind == 1)
        def _():
            backward(m)

        @pl.when(kind == 2)
        def _():
            prepare(m)

        @pl.when(kind == 3)
        def _():
            accumulate(m)

    result = pltpu.make_async_copy(grad, out, out_sem)
    result.start()

    @pl.loop(0, micros)
    def _(m):
        slope_edge(m).wait_send()
        for j in range(3):
            x_slice(m, j).wait_send()
        for c in range(2):
            for j in range(3):
                d_block(m, c, j).wait_send()

            @pl.when(stage < last)
            def _():
                x_main(m, c).wait_send()
                x_edge(m, c).wait_send()

            @pl.when(stage == 0)
            def _():
                x_first(m, c).wait_send()

            @pl.when(stage > 0)
            def _():
                g_main(m, c).wait_send()
                g_edge(m, c).wait_send()

            @pl.when(stage == last)
            def _():
                g_first(m, c).wait_send()

    result.wait()


def kernel_shards(images, cotangent, weights):
    micros, imgs, rows, cols, chans = images.shape
    quarters = chans // LANES
    pixels = rows * cols
    bf16, f32 = jnp.bfloat16, jnp.float32
    dma = pltpu.SemaphoreType.DMA
    padded = (micros, quarters, rows + 2, cols, LANES)
    plain = (micros, quarters, rows, cols, LANES)
    flops = 2 * 3 * micros * pixels * 9 * chans * chans
    grads = pl.pallas_call(
        pipeline_kernel,
        out_shape=jax.ShapeDtypeStruct((9, LANES, chans), f32),
        in_specs=[pl.BlockSpec(memory_space=pl.ANY)] * 3,
        out_specs=pl.BlockSpec(memory_space=pl.ANY),
        scratch_shapes=[
            pltpu.VMEM((9, chans, chans), bf16),
            pltpu.VMEM((9, chans, chans), bf16),
            pltpu.VMEM(padded, bf16),
            pltpu.VMEM(plain, bf16),
            pltpu.VMEM(padded, bf16),
            pltpu.VMEM(plain, bf16),
            pltpu.VMEM(padded, f32),
            pltpu.VMEM((micros, 4, quarters, pixels, LANES), bf16),
            pltpu.VMEM((micros, 4, rows, cols, LANES), bf16),
            pltpu.VMEM((micros, 2, 9, LANES, 2 * pixels), bf16),
            pltpu.VMEM((pixels, chans), f32),
            pltpu.VMEM((2, rows + 2, cols, 3 * chans // 2), bf16),
            pltpu.VMEM((9, LANES, chans), f32),
            dma, dma((micros, quarters)), dma,
            dma((micros, 2)),
            dma((micros, 2)), dma((micros, 2)), dma((micros, 2)), dma((micros, 2)),
            dma((micros, 2)), dma((micros, 2)), dma((micros, 2)), dma((micros, 2)),
            dma((micros,)), dma((micros,)), dma((micros, 3)), dma((micros, 3)),
            dma((micros, 3, 2)), dma((micros, 3, 2)),
        ],
        compiler_params=pltpu.CompilerParams(
            collective_id=0, has_side_effects=True, vmem_limit_bytes=48 * 2**20),
        cost_estimate=pl.CostEstimate(
            flops=flops, bytes_accessed=2 * 9 * chans * chans * 2, transcendentals=0),
    )(
        images.reshape(micros, rows, cols, chans),
        cotangent.reshape(micros, rows, cols, chans),
        weights.reshape(9, chans, chans),
    )
    return grads[None]


def solution(mesh):
    placed = (
        P(None, "dp", "spatial", None, None),
        P(None, "dp", "spatial", None, None),
        P("chain", None, None, None),
    )

    def program(images, cotangent, weights):
        group = mesh.shape["spatial"] * mesh.shape["dp"]
        fits = (
            mesh.shape["spatial"] == 2
            and mesh.shape["dp"] == 2
            and images.shape[1] == 2
            and weights.shape[2] == group * LANES
            and images.shape[2] * images.shape[3] == 2 * LANES
        )
        return jax.shard_map(
            kernel_shards if fits else shards,
            mesh=mesh,
            in_specs=placed,
            out_specs=P("chain", None, ("spatial", "dp"), None),
            check_vma=False,
        )(images, cotangent, weights)

    return program
```

```python
import jax
import jax.numpy as jnp
from jax import lax
from jax.experimental import pallas as pl
from jax.experimental.pallas import tpu as pltpu
from jax.sharding import PartitionSpec as P


def with_halo(cells, sides, width):
    for axis, dim in sides:
        count = lax.axis_size(axis)
        ends = count - 1
        head = lax.slice_in_dim(cells, 0, width, axis=dim)
        tail = lax.slice_in_dim(cells, cells.shape[dim] - width, cells.shape[dim], axis=dim)
        cells = jnp.concatenate(
            [
                lax.ppermute(tail, axis, [(i, (i + 1) % count) for i in range(ends)]),
                cells,
                lax.ppermute(head, axis, [((i + 1) % count, i) for i in range(ends)]),
            ],
            axis=dim,
        )
    return cells


def passed_along(block, axis, distance):
    devices = range(lax.axis_size(axis))
    route = [(i - distance, i) for i in devices if i - distance in devices]
    return lax.ppermute(block, axis, route)


def patches(padded, rows, cols, reverse):
    offsets = [(a, b) for a in range(3) for b in range(3)]
    if reverse:
        offsets = offsets[::-1]
    parts = [padded[:, a : a + rows, b : b + cols, :] for a, b in offsets]
    return jnp.stack(parts, axis=-2).reshape(-1, 9, padded.shape[-1])


def pad_cols(field):
    return jnp.pad(field, ((0, 0), (0, 0), (1, 1), (0, 0)))


def silu_slope(value):
    sig = jax.nn.sigmoid(value)
    return sig * (1.0 + value * (1.0 - sig))


def shards(images, cotangent, weights):
    micros, imgs, height, width, chans = images.shape
    pixels = imgs * height * width
    sections = lax.axis_size("chain")
    section = lax.axis_index("chain")
    ticks = micros + sections - 1
    kernel = weights[0]
    flat_kernel = kernel.reshape(9 * chans, chans)
    shape_one = (imgs, height, width, chans)

    def forward_tick(tick, carry):
        inbox, saved_x, saved_z = carry
        micro = tick - section
        valid = jnp.logical_and(micro >= 0, micro < micros)
        slot = jnp.clip(micro, 0, micros - 1)
        first = lax.dynamic_index_in_dim(images, slot, 0, keepdims=False)
        source = jnp.where(section == 0, first, inbox)
        rows = with_halo(source, (("spatial", 1),), 1)
        padded = pad_cols(rows)

        def forward_active(operand):
            cols = patches(operand, height, width, False).reshape(-1, 9 * chans)
            state = jnp.dot(cols, flat_kernel, preferred_element_type=jnp.float32)
            output = (source.astype(jnp.float32) + jax.nn.silu(state).reshape(shape_one)).astype(
                jnp.bfloat16
            )
            return (output, state)

        def forward_resting(operand):
            return (jnp.zeros(shape_one, jnp.bfloat16), jnp.zeros((pixels, chans), jnp.float32))

        output, state = lax.cond(valid, forward_active, forward_resting, padded)
        saved_x = jnp.where(
            valid, lax.dynamic_update_index_in_dim(saved_x, padded, slot, 0), saved_x
        )
        saved_z = jnp.where(
            valid, lax.dynamic_update_index_in_dim(saved_z, state, slot, 0), saved_z
        )
        inbox = passed_along(output, "chain", 1)
        return (inbox, saved_x, saved_z)

    start = (
        jnp.zeros(shape_one, jnp.bfloat16),
        jnp.zeros((micros, imgs, height + 2, width + 2, chans), jnp.bfloat16),
        jnp.zeros((micros, pixels, chans), jnp.float32),
    )
    inbox, saved_x, saved_z = lax.fori_loop(0, ticks, forward_tick, start)

    def backward_tick(tick, carry):
        inbox, saved_d = carry
        micro = tick - (sections - 1 - section)
        valid = jnp.logical_and(micro >= 0, micro < micros)
        slot = jnp.clip(micro, 0, micros - 1)
        last = lax.dynamic_index_in_dim(cotangent, slot, 0, keepdims=False)
        upstream = jnp.where(section == sections - 1, last, inbox)
        state = lax.dynamic_index_in_dim(saved_z, slot, 0, keepdims=False)
        delta = (upstream.astype(jnp.float32).reshape(pixels, chans) * silu_slope(state)).astype(
            jnp.bfloat16
        )
        delta = jnp.where(valid, delta, jnp.zeros_like(delta))
        rows = with_halo(delta.reshape(shape_one), (("spatial", 1),), 1)
        padded = pad_cols(rows)

        def backward_active(operand):
            back = patches(operand, height, width, True)
            flow = jnp.einsum("nkc,kdc->nd", back, kernel, preferred_element_type=jnp.float32)
            return (upstream.astype(jnp.float32) + flow.reshape(shape_one)).astype(jnp.bfloat16)

        def backward_resting(operand):
            return jnp.zeros(shape_one, jnp.bfloat16)

        result = lax.cond(valid, backward_active, backward_resting, padded)
        saved_d = jnp.where(
            valid, lax.dynamic_update_index_in_dim(saved_d, delta, slot, 0), saved_d
        )
        inbox = passed_along(result, "chain", -1)
        return (inbox, saved_d)

    begin = (jnp.zeros(shape_one, jnp.bfloat16), jnp.zeros((micros, pixels, chans), jnp.bfloat16))
    inbox, saved_d = lax.fori_loop(0, ticks, backward_tick, begin)
    cols_all = patches(
        saved_x.reshape(micros * imgs, height + 2, width + 2, chans), height, width, False
    )
    cols_all = cols_all.reshape(-1, 9 * chans)
    local_grad = lax.dot_general(
        cols_all,
        saved_d.reshape(-1, chans),
        (((0,), (0,)), ((), ())),
        preferred_element_type=jnp.float32,
    ).reshape(9, chans, chans)
    summed = lax.psum_scatter(
        local_grad.astype(jnp.bfloat16), ("spatial", "dp"), scatter_dimension=1, tiled=True
    ).astype(jnp.float32)
    return summed[None]

LANES = 128
MESH = pl.DeviceIdType.MESH


def pipeline_kernel(
    images, cotangent, weights, out,
    w, wt, first, xin, xout, gin, gout, slope, dall, xs, xt, acc, cat, grad,
    w_sem, loc_sem, out_sem,
    f_send, fm_send, x_send, x_recv, xh_send, xh_recv,
    g_send, g_recv, gh_send, gh_recv,
    s_send, s_recv, xs_send, xs_recv, d_send, d_recv,
):
    micros, quarters, padded_rows, cols, _ = xin.shape
    rows = padded_rows - 2
    pixels = rows * cols
    chans = quarters * LANES
    half = chans // 2
    hq = quarters // 2
    stage = lax.axis_index("chain")
    last = lax.axis_size("chain") - 1
    sp = lax.axis_index("spatial")
    dp = lax.axis_index("dp")
    osp, odp = 1 - sp, 1 - dp
    me = sp * 2 + dp
    mates = ((sp, odp), (osp, dp), (osp, odp))
    edge_src = (rows - 1) * odp
    edge_dst = (rows + 1) * dp
    moved = sp != dp

    def remote(src, dst, send, recv, chain, spatial, core):
        return pltpu.make_async_remote_copy(
            src_ref=src, dst_ref=dst, send_sem=send, recv_sem=recv,
            device_id=(chain, spatial, core), device_id_type=MESH,
        )

    def x_main(m, c):
        return remote(
            xout.at[m, pl.ds(c * hq, hq)], xin.at[m, pl.ds(c * hq, hq), pl.ds(1, rows)],
            x_send.at[m, c], x_recv.at[m, c], stage + 1, sp, dp)

    def x_edge(m, c):
        return remote(
            xout.at[m, pl.ds(c * hq, hq), pl.ds(edge_src, 1)],
            xin.at[m, pl.ds(c * hq, hq), pl.ds(edge_dst, 1)],
            xh_send.at[m, c], xh_recv.at[m, c], stage + 1, sp, odp)

    def first_main(buffer, recv, m, c):
        return remote(
            first.at[m, pl.ds(c * hq, hq)], buffer.at[m, pl.ds(c * hq, hq), pl.ds(1, rows)],
            fm_send.at[m, c], recv.at[m, c], stage, dp, sp)

    def first_edge(buffer, recv, m, c):
        return remote(
            first.at[m, pl.ds(c * hq, hq), pl.ds((rows - 1) * osp, 1)],
            buffer.at[m, pl.ds(c * hq, hq), pl.ds((rows + 1) * sp, 1)],
            f_send.at[m, c], recv.at[m, c], stage, dp, osp)

    def g_main(m, c):
        return remote(
            gout.at[m, pl.ds(c * hq, hq)], gin.at[m, pl.ds(c * hq, hq), pl.ds(1, rows)],
            g_send.at[m, c], g_recv.at[m, c], stage - 1, sp, dp)

    def g_edge(m, c):
        return remote(
            gout.at[m, pl.ds(c * hq, hq), pl.ds(edge_src, 1)],
            gin.at[m, pl.ds(c * hq, hq), pl.ds(edge_dst, 1)],
            gh_send.at[m, c], gh_recv.at[m, c], stage - 1, sp, odp)

    def slope_edge(m):
        return remote(
            slope.at[m, :, pl.ds(1 + edge_src, 1)], slope.at[m, :, pl.ds(edge_dst, 1)],
            s_send.at[m], s_recv.at[m], stage, sp, odp)

    def x_slice(m, j):
        a, b = mates[j]
        return remote(
            xin.at[m, a * 2 + b, pl.ds(1, rows)], xs.at[m, me],
            xs_send.at[m, j], xs_recv.at[m, j], stage, a, b)

    def d_block(m, c, j):
        a, b = ((sp, odp), (osp, dp), (sp, odp))[j]
        owner = me if j < 2 else osp * 2 + dp
        block = dall.at[m, owner, pl.ds(c * hq, hq)]
        return remote(block, block, d_send.at[m, j, c], d_recv.at[m, j, c], stage, a, b)

    def local_in(array, m, q):
        return pltpu.make_async_copy(
            array.at[m, :, :, pl.ds(q * LANES, LANES)], first.at[m, q], loc_sem.at[m, q])

    def hand_out(array, buffer, recv, edge_recv):
        for m in range(micros):
            for q in range(quarters):
                local_in(array, m, q).wait()

            @pl.when(moved)
            def _():
                for c in range(2):
                    first_main(buffer, recv, m, c).start()

            for c in range(2):
                first_edge(buffer, edge_recv, m, c).start()

            @pl.when(jnp.logical_not(moved))
            def _():
                buffer[m, :, pl.ds(1, rows)] = first[m]

    w_copy = pltpu.make_async_copy(weights, w, w_sem)
    w_copy.start()

    @pl.when(stage == 0)
    def _():
        for m in range(micros):
            for q in range(quarters):
                local_in(images, m, q).start()

    @pl.when(stage == last)
    def _():
        for m in range(micros):
            for q in range(quarters):
                local_in(cotangent, m, q).start()

    barrier = pltpu.get_barrier_semaphore()

    def greet(chain, spatial, core):
        pl.semaphore_signal(barrier, inc=1, device_id=(chain, spatial, core), device_id_type=MESH)

    for a, b in mates:
        greet(stage, a, b)

    @pl.when(stage > 0)
    def _():
        greet(stage - 1, sp, dp)
        greet(stage - 1, sp, odp)

    @pl.when(stage < last)
    def _():
        greet(stage + 1, sp, dp)
        greet(stage + 1, sp, odp)

    zero_row = (rows + 1) * dp
    blank = jnp.zeros((micros, quarters, 1, cols, LANES), jnp.float32)
    xin[:, :, pl.ds(zero_row, 1)] = blank.astype(xin.dtype)
    gin[:, :, pl.ds(zero_row, 1)] = blank.astype(gin.dtype)
    slope[:, :, pl.ds(zero_row, 1)] = blank
    grad[...] = jnp.zeros_like(grad)

    around = jnp.where(stage > 0, 2, 0) + jnp.where(stage < last, 2, 0)
    pl.semaphore_wait(barrier, 3 + around)

    @pl.when(stage == 0)
    def _():
        hand_out(images, xin, x_recv, xh_recv)

    @pl.when(stage == last)
    def _():
        hand_out(cotangent, gin, g_recv, gh_recv)

    w_copy.wait()

    @pl.when(stage > 0)
    def _():
        @pl.loop(0, 9)
        def _(k):
            wt[k] = w[8 - k].T

    def column_shifts(value):
        n = value.shape[0]
        col = lax.broadcasted_iota(jnp.int32, value.shape, 0) % cols
        before = jnp.where(col == 0, 0.0, pltpu.roll(value, 1, 0))
        after = jnp.where(col == cols - 1, 0.0, pltpu.roll(value, n - 1, 0))
        return before, value, after

    def load_half(ref, m, c):
        parts = [ref[m, c * hq + i].astype(jnp.float32) for i in range(hq)]
        return jnp.concatenate(parts, axis=-1)

    def spread(value, c):
        shifted = column_shifts(value.reshape(padded_rows * cols, half))
        joined = jnp.concatenate([v.astype(cat.dtype) for v in shifted], axis=-1)
        cat[c] = joined.reshape(padded_rows, cols, 3 * half)

    def product(kernel, c, lo, width):
        lhs = jnp.concatenate(
            [cat[c, pl.ds(a, rows)].reshape(pixels, 3 * half) for a in range(3)], axis=-1)
        rhs = kernel[:, pl.ds(c * half, half), pl.ds(lo, width)].reshape(9 * half, width)
        return jnp.dot(lhs, rhs, preferred_element_type=jnp.float32)

    def store_half(ref, m, n, first, value):
        for i in range(hq):
            part = value[:, i * LANES:(i + 1) * LANES].reshape(rows, cols, LANES)
            ref[m, n * hq + i, pl.ds(first, rows)] = part.astype(ref.dtype)

    def forward(m):
        for c in range(2):
            @pl.when(jnp.logical_or(stage > 0, moved))
            def _():
                x_main(m, c).wait_recv()

            x_edge(m, c).wait_recv()
            spread(load_half(xin, m, c), c)
            if c == 0:
                acc[...] = product(w, 0, 0, chans)
        for n in range(2):
            z = acc[:, pl.ds(n * half, half)] + product(w, 1, n * half, half)
            sig = jax.nn.sigmoid(z)
            own = load_half(xin, m, n)[1:rows + 1].reshape(pixels, half)
            store_half(xout, m, n, 0, own + z * sig)

            @pl.when(stage < last)
            def _():
                x_main(m, n).start()
                x_edge(m, n).start()

            store_half(slope, m, n, 1, sig * (1.0 + z * (1.0 - sig)))
        slope_edge(m).start()
        for j in range(3):
            x_slice(m, j).start()
        xs[m, me] = xin[m, me, pl.ds(1, rows)]

    def backward(m):
        slope_edge(m).wait_recv()
        for c in range(2):
            @pl.when(jnp.logical_or(stage < last, moved))
            def _():
                g_main(m, c).wait_recv()

            g_edge(m, c).wait_recv()

            d = (load_half(gin, m, c) * load_half(slope, m, c)).astype(dall.dtype)
            for i in range(hq):
                dall[m, me, c * hq + i] = d[1:rows + 1, :, i * LANES:(i + 1) * LANES].reshape(
                    pixels, LANES)
            @pl.when(stage > 0)
            def _():
                spread(d.astype(jnp.float32), c)
                if c == 0:
                    acc[...] = product(wt, 0, 0, chans)

            d_block(m, c, 1).start()
            d_block(m, c, 0).start()

        @pl.when(stage > 0)
        def _():
            for n in range(2):
                own = load_half(gin, m, n)[1:rows + 1].reshape(pixels, half)
                flow = acc[:, pl.ds(n * half, half)] + product(wt, 1, n * half, half)
                store_half(gout, m, n, 0, own + flow)
                g_main(m, n).start()
                g_edge(m, n).start()

        @pl.when(m > 0)
        def _():
            pass_on(m - 1)

    def prepare(m):
        for j in range(3):
            x_slice(m, j).wait_recv()
        for image in range(2):
            tall = jnp.concatenate([xs[m, 2 * image], xs[m, 2 * image + 1]], axis=0).astype(jnp.float32)
            blank_row = jnp.zeros((1, cols, LANES), jnp.float32)
            shifted = column_shifts(tall.reshape(2 * pixels, LANES))
            for b in range(3):
                field = jnp.concatenate(
                    [blank_row, shifted[b].reshape(2 * rows, cols, LANES), blank_row], axis=0)
                for part in range(2):
                    for a in range(3):
                        lo = part * rows + a
                        block = field[lo:lo + rows].reshape(pixels, LANES)
                        xt[m, image, 3 * a + b, :, pl.ds(part * LANES, LANES)] = block.T.astype(
                            xt.dtype)

    def add_grad(m, image):
        blocks = []
        for part in range(2):
            blocks.append(jnp.concatenate(
                [dall[m, image * 2 + part, q] for q in range(quarters)], axis=-1))
        rhs = jnp.concatenate(blocks, axis=0)
        for a in range(3):
            lhs = xt[m, image, pl.ds(3 * a, 3)].reshape(3 * LANES, 2 * pixels)
            total = jnp.dot(lhs, rhs, preferred_element_type=jnp.float32)
            grad[pl.ds(3 * a, 3)] += total.reshape(3, LANES, chans)

    def pass_on(m):
        for c in range(2):
            d_block(m, c, 1).wait_recv()
            d_block(m, c, 2).start()

    def accumulate(m):
        @pl.when(m == micros - 1)
        def _():
            pass_on(m)

        for c in range(2):
            d_block(m, c, 0).wait_recv()
        add_grad(m, sp)
        for c in range(2):
            d_block(m, c, 2).wait_recv()
        add_grad(m, osp)

    F, B, Q, W = ([k * micros + i for i in range(micros)] for k in range(4))
    early = F + Q + [B[0]]
    for i in range(1, micros):
        early += [B[i], W[i - 1]]
    early += [W[-1]]
    late = F + B + Q + W
    final = [v for pair in zip(F, B) for v in pair] + Q + W

    @pl.loop(0, 4 * micros)
    def _(step):
        code = jnp.int32(0)
        for i in range(4 * micros):
            choice = jnp.where(
                stage == last, final[i], jnp.where(stage * 2 < last + 1, early[i], late[i]))
            code = jnp.where(step == i, choice, code)
        kind = code // micros
        m = code % micros

        @pl.when(kind == 0)
        def _():
            forward(m)

        @pl.when(kind == 1)
        def _():
            backward(m)

        @pl.when(kind == 2)
        def _():
            prepare(m)

        @pl.when(kind == 3)
        def _():
            accumulate(m)

    result = pltpu.make_async_copy(grad, out, out_sem)
    result.start()

    @pl.loop(0, micros)
    def _(m):
        slope_edge(m).wait_send()
        for j in range(3):
            x_slice(m, j).wait_send()
        for c in range(2):
            for j in range(3):
                d_block(m, c, j).wait_send()

            @pl.when(stage < last)
            def _():
                x_main(m, c).wait_send()
                x_edge(m, c).wait_send()

            @pl.when(stage > 0)
            def _():
                g_main(m, c).wait_send()
                g_edge(m, c).wait_send()

            @pl.when(jnp.logical_or(stage == 0, stage == last))
            def _():
                first_edge(xin, xh_recv, m, c).wait_send()

                @pl.when(moved)
                def _():
                    first_main(xin, x_recv, m, c).wait_send()

    result.wait()


def kernel_shards(images, cotangent, weights):
    micros, imgs, rows, cols, chans = images.shape
    quarters = chans // LANES
    pixels = rows * cols
    bf16, f32 = jnp.bfloat16, jnp.float32
    dma = pltpu.SemaphoreType.DMA
    padded = (micros, quarters, rows + 2, cols, LANES)
    plain = (micros, quarters, rows, cols, LANES)
    flops = 2 * 3 * micros * pixels * 9 * chans * chans
    grads = pl.pallas_call(
        pipeline_kernel,
        out_shape=jax.ShapeDtypeStruct((9, LANES, chans), f32),
        in_specs=[pl.BlockSpec(memory_space=pltpu.HBM)] * 3,
        out_specs=pl.BlockSpec(memory_space=pl.ANY),
        scratch_shapes=[
            pltpu.VMEM((9, chans, chans), bf16),
            pltpu.VMEM((9, chans, chans), bf16),
            pltpu.VMEM(plain, bf16),
            pltpu.VMEM(padded, bf16),
            pltpu.VMEM(plain, bf16),
            pltpu.VMEM(padded, bf16),
            pltpu.VMEM(plain, bf16),
            pltpu.VMEM(padded, f32),
            pltpu.VMEM((micros, 4, quarters, pixels, LANES), bf16),
            pltpu.VMEM((micros, 4, rows, cols, LANES), bf16),
            pltpu.VMEM((micros, 2, 9, LANES, 2 * pixels), bf16),
            pltpu.VMEM((pixels, chans), f32),
            pltpu.VMEM((2, rows + 2, cols, 3 * chans // 2), bf16),
            pltpu.VMEM((9, LANES, chans), f32),
            dma, dma((micros, quarters)), dma,
            dma((micros, 2)), dma((micros, 2)),
            dma((micros, 2)), dma((micros, 2)), dma((micros, 2)), dma((micros, 2)),
            dma((micros, 2)), dma((micros, 2)), dma((micros, 2)), dma((micros, 2)),
            dma((micros,)), dma((micros,)), dma((micros, 3)), dma((micros, 3)),
            dma((micros, 3, 2)), dma((micros, 3, 2)),
        ],
        compiler_params=pltpu.CompilerParams(
            collective_id=0, has_side_effects=True, vmem_limit_bytes=48 * 2**20),
        cost_estimate=pl.CostEstimate(
            flops=flops, bytes_accessed=2 * 9 * chans * chans * 2, transcendentals=0),
    )(
        images.reshape(micros, rows, cols, chans),
        cotangent.reshape(micros, rows, cols, chans),
        weights.reshape(9, chans, chans),
    )
    return grads[None]


def solution(mesh):
    placed = (
        P(None, "dp", "spatial", None, None),
        P(None, "dp", "spatial", None, None),
        P("chain", None, None, None),
    )

    def program(images, cotangent, weights):
        group = mesh.shape["spatial"] * mesh.shape["dp"]
        fits = (
            mesh.shape["spatial"] == 2
            and mesh.shape["dp"] == 2
            and images.shape[1] == 2
            and weights.shape[2] == group * LANES
            and images.shape[2] * images.shape[3] == 2 * LANES
        )
        return jax.shard_map(
            kernel_shards if fits else shards,
            mesh=mesh,
            in_specs=placed,
            out_specs=P("chain", None, ("spatial", "dp"), None),
            check_vma=False,
        )(images, cotangent, weights)

    return program
```

```python
import jax
import jax.numpy as jnp
from jax import lax
from jax.experimental import pallas as pl
from jax.experimental.pallas import tpu as pltpu
from jax.sharding import PartitionSpec as P


def with_halo(cells, sides, width):
    for axis, dim in sides:
        count = lax.axis_size(axis)
        ends = count - 1
        head = lax.slice_in_dim(cells, 0, width, axis=dim)
        tail = lax.slice_in_dim(cells, cells.shape[dim] - width, cells.shape[dim], axis=dim)
        cells = jnp.concatenate(
            [
                lax.ppermute(tail, axis, [(i, (i + 1) % count) for i in range(ends)]),
                cells,
                lax.ppermute(head, axis, [((i + 1) % count, i) for i in range(ends)]),
            ],
            axis=dim,
        )
    return cells


def passed_along(block, axis, distance):
    devices = range(lax.axis_size(axis))
    route = [(i - distance, i) for i in devices if i - distance in devices]
    return lax.ppermute(block, axis, route)


def patches(padded, rows, cols, reverse):
    offsets = [(a, b) for a in range(3) for b in range(3)]
    if reverse:
        offsets = offsets[::-1]
    parts = [padded[:, a : a + rows, b : b + cols, :] for a, b in offsets]
    return jnp.stack(parts, axis=-2).reshape(-1, 9, padded.shape[-1])


def pad_cols(field):
    return jnp.pad(field, ((0, 0), (0, 0), (1, 1), (0, 0)))


def silu_slope(value):
    sig = jax.nn.sigmoid(value)
    return sig * (1.0 + value * (1.0 - sig))


def shards(images, cotangent, weights):
    micros, imgs, height, width, chans = images.shape
    pixels = imgs * height * width
    sections = lax.axis_size("chain")
    section = lax.axis_index("chain")
    ticks = micros + sections - 1
    kernel = weights[0]
    flat_kernel = kernel.reshape(9 * chans, chans)
    shape_one = (imgs, height, width, chans)

    def forward_tick(tick, carry):
        inbox, saved_x, saved_z = carry
        micro = tick - section
        valid = jnp.logical_and(micro >= 0, micro < micros)
        slot = jnp.clip(micro, 0, micros - 1)
        first = lax.dynamic_index_in_dim(images, slot, 0, keepdims=False)
        source = jnp.where(section == 0, first, inbox)
        rows = with_halo(source, (("spatial", 1),), 1)
        padded = pad_cols(rows)

        def forward_active(operand):
            cols = patches(operand, height, width, False).reshape(-1, 9 * chans)
            state = jnp.dot(cols, flat_kernel, preferred_element_type=jnp.float32)
            output = (source.astype(jnp.float32) + jax.nn.silu(state).reshape(shape_one)).astype(
                jnp.bfloat16
            )
            return (output, state)

        def forward_resting(operand):
            return (jnp.zeros(shape_one, jnp.bfloat16), jnp.zeros((pixels, chans), jnp.float32))

        output, state = lax.cond(valid, forward_active, forward_resting, padded)
        saved_x = jnp.where(
            valid, lax.dynamic_update_index_in_dim(saved_x, padded, slot, 0), saved_x
        )
        saved_z = jnp.where(
            valid, lax.dynamic_update_index_in_dim(saved_z, state, slot, 0), saved_z
        )
        inbox = passed_along(output, "chain", 1)
        return (inbox, saved_x, saved_z)

    start = (
        jnp.zeros(shape_one, jnp.bfloat16),
        jnp.zeros((micros, imgs, height + 2, width + 2, chans), jnp.bfloat16),
        jnp.zeros((micros, pixels, chans), jnp.float32),
    )
    inbox, saved_x, saved_z = lax.fori_loop(0, ticks, forward_tick, start)

    def backward_tick(tick, carry):
        inbox, saved_d = carry
        micro = tick - (sections - 1 - section)
        valid = jnp.logical_and(micro >= 0, micro < micros)
        slot = jnp.clip(micro, 0, micros - 1)
        last = lax.dynamic_index_in_dim(cotangent, slot, 0, keepdims=False)
        upstream = jnp.where(section == sections - 1, last, inbox)
        state = lax.dynamic_index_in_dim(saved_z, slot, 0, keepdims=False)
        delta = (upstream.astype(jnp.float32).reshape(pixels, chans) * silu_slope(state)).astype(
            jnp.bfloat16
        )
        delta = jnp.where(valid, delta, jnp.zeros_like(delta))
        rows = with_halo(delta.reshape(shape_one), (("spatial", 1),), 1)
        padded = pad_cols(rows)

        def backward_active(operand):
            back = patches(operand, height, width, True)
            flow = jnp.einsum("nkc,kdc->nd", back, kernel, preferred_element_type=jnp.float32)
            return (upstream.astype(jnp.float32) + flow.reshape(shape_one)).astype(jnp.bfloat16)

        def backward_resting(operand):
            return jnp.zeros(shape_one, jnp.bfloat16)

        result = lax.cond(valid, backward_active, backward_resting, padded)
        saved_d = jnp.where(
            valid, lax.dynamic_update_index_in_dim(saved_d, delta, slot, 0), saved_d
        )
        inbox = passed_along(result, "chain", -1)
        return (inbox, saved_d)

    begin = (jnp.zeros(shape_one, jnp.bfloat16), jnp.zeros((micros, pixels, chans), jnp.bfloat16))
    inbox, saved_d = lax.fori_loop(0, ticks, backward_tick, begin)
    cols_all = patches(
        saved_x.reshape(micros * imgs, height + 2, width + 2, chans), height, width, False
    )
    cols_all = cols_all.reshape(-1, 9 * chans)
    local_grad = lax.dot_general(
        cols_all,
        saved_d.reshape(-1, chans),
        (((0,), (0,)), ((), ())),
        preferred_element_type=jnp.float32,
    ).reshape(9, chans, chans)
    summed = lax.psum_scatter(
        local_grad.astype(jnp.bfloat16), ("spatial", "dp"), scatter_dimension=1, tiled=True
    ).astype(jnp.float32)
    return summed[None]

LANES = 128
MESH = pl.DeviceIdType.MESH


def pipeline_kernel(
    images, cotangent, weights, out,
    w, wt, xin, xout, gin, gout, slope, dall, xs, xt, acc, cat, grad,
    w_sem, loc_sem, out_sem,
    f_send, x_send, x_recv, xh_send, xh_recv,
    g_send, g_recv, gh_send, gh_recv,
    s_send, s_recv, xs_send, xs_recv, d_send, d_recv,
):
    micros, quarters, padded_rows, cols, _ = xin.shape
    rows = padded_rows - 2
    pixels = rows * cols
    chans = quarters * LANES
    half = chans // 2
    hq = quarters // 2
    stage = lax.axis_index("chain")
    last = lax.axis_size("chain") - 1
    sp = lax.axis_index("spatial")
    dp = lax.axis_index("dp")
    osp, odp = 1 - sp, 1 - dp
    me = sp * 2 + dp
    mates = ((sp, odp), (osp, dp), (osp, odp))
    edge_src = (rows - 1) * osp
    edge_dst = (rows + 1) * sp

    def remote(src, dst, send, recv, chain, spatial, core):
        return pltpu.make_async_remote_copy(
            src_ref=src, dst_ref=dst, send_sem=send, recv_sem=recv,
            device_id=(chain, spatial, core), device_id_type=MESH,
        )

    def x_main(m, c):
        return remote(
            xout.at[m, pl.ds(c * hq, hq)], xin.at[m, pl.ds(c * hq, hq), pl.ds(1, rows)],
            x_send.at[m, c], x_recv.at[m, c], stage + 1, sp, dp)

    def x_edge(m, c):
        return remote(
            xout.at[m, pl.ds(c * hq, hq), pl.ds(edge_src, 1)],
            xin.at[m, pl.ds(c * hq, hq), pl.ds(edge_dst, 1)],
            xh_send.at[m, c], xh_recv.at[m, c], stage + 1, osp, dp)

    def x_first(m, c):
        return remote(
            xin.at[m, pl.ds(c * hq, hq), pl.ds(1 + edge_src, 1)],
            xin.at[m, pl.ds(c * hq, hq), pl.ds(edge_dst, 1)],
            f_send.at[m, c], xh_recv.at[m, c], stage, osp, dp)

    def g_main(m, c):
        return remote(
            gout.at[m, pl.ds(c * hq, hq)], gin.at[m, pl.ds(c * hq, hq), pl.ds(1, rows)],
            g_send.at[m, c], g_recv.at[m, c], stage - 1, sp, dp)

    def g_edge(m, c):
        return remote(
            gout.at[m, pl.ds(c * hq, hq), pl.ds(edge_src, 1)],
            gin.at[m, pl.ds(c * hq, hq), pl.ds(edge_dst, 1)],
            gh_send.at[m, c], gh_recv.at[m, c], stage - 1, osp, dp)

    def g_first(m, c):
        return remote(
            gin.at[m, pl.ds(c * hq, hq), pl.ds(1 + edge_src, 1)],
            gin.at[m, pl.ds(c * hq, hq), pl.ds(edge_dst, 1)],
            f_send.at[m, c], gh_recv.at[m, c], stage, osp, dp)

    def slope_edge(m):
        return remote(
            slope.at[m, :, pl.ds(1 + edge_src, 1)], slope.at[m, :, pl.ds(edge_dst, 1)],
            s_send.at[m], s_recv.at[m], stage, osp, dp)

    def x_slice(m, j):
        a, b = mates[j]
        return remote(
            xin.at[m, a * 2 + b, pl.ds(1, rows)], xs.at[m, me],
            xs_send.at[m, j], xs_recv.at[m, j], stage, a, b)

    def d_block(m, c, j):
        a, b = ((sp, odp), (osp, dp), (sp, odp))[j]
        owner = me if j < 2 else osp * 2 + dp
        block = dall.at[m, owner, pl.ds(c * hq, hq)]
        return remote(block, block, d_send.at[m, j, c], d_recv.at[m, j, c], stage, a, b)

    def local_in(array, buffer, m, q):
        return pltpu.make_async_copy(
            array.at[m, :, :, pl.ds(q * LANES, LANES)], buffer.at[m, q, pl.ds(1, rows)],
            loc_sem.at[m, q])

    w_copy = pltpu.make_async_copy(weights, w, w_sem)
    w_copy.start()

    @pl.when(stage == 0)
    def _():
        for m in range(micros):
            for q in range(quarters):
                local_in(images, xin, m, q).start()

    @pl.when(stage == last)
    def _():
        for m in range(micros):
            for q in range(quarters):
                local_in(cotangent, gin, m, q).start()

    barrier = pltpu.get_barrier_semaphore()

    def greet(chain, spatial, core):
        pl.semaphore_signal(barrier, inc=1, device_id=(chain, spatial, core), device_id_type=MESH)

    for a, b in mates:
        greet(stage, a, b)

    @pl.when(stage > 0)
    def _():
        greet(stage - 1, sp, dp)
        greet(stage - 1, osp, dp)

    @pl.when(stage < last)
    def _():
        greet(stage + 1, sp, dp)
        greet(stage + 1, osp, dp)

    zero_row = (rows + 1) * sp
    blank = jnp.zeros((micros, quarters, 1, cols, LANES), jnp.float32)
    xin[:, :, pl.ds(zero_row, 1)] = blank.astype(xin.dtype)
    gin[:, :, pl.ds(zero_row, 1)] = blank.astype(gin.dtype)
    slope[:, :, pl.ds(zero_row, 1)] = blank
    grad[...] = jnp.zeros_like(grad)

    around = jnp.where(stage > 0, 2, 0) + jnp.where(stage < last, 2, 0)
    pl.semaphore_wait(barrier, 3 + around)

    @pl.when(stage == 0)
    def _():
        for m in range(micros):
            for q in range(quarters):
                local_in(images, xin, m, q).wait()
            for c in range(2):
                x_first(m, c).start()

    @pl.when(stage == last)
    def _():
        for m in range(micros):
            for q in range(quarters):
                local_in(cotangent, gin, m, q).wait()
            for c in range(2):
                g_first(m, c).start()

    w_copy.wait()

    @pl.when(stage > 0)
    def _():
        @pl.loop(0, 9)
        def _(k):
            wt[k] = w[8 - k].T

    def column_shifts(value):
        n = value.shape[0]
        col = lax.broadcasted_iota(jnp.int32, value.shape, 0) % cols
        before = jnp.where(col == 0, 0.0, pltpu.roll(value, 1, 0))
        after = jnp.where(col == cols - 1, 0.0, pltpu.roll(value, n - 1, 0))
        return before, value, after

    def load_half(ref, m, c):
        parts = [ref[m, c * hq + i].astype(jnp.float32) for i in range(hq)]
        return jnp.concatenate(parts, axis=-1)

    def spread(value, c):
        shifted = column_shifts(value.reshape(padded_rows * cols, half))
        joined = jnp.concatenate([v.astype(cat.dtype) for v in shifted], axis=-1)
        cat[c] = joined.reshape(padded_rows, cols, 3 * half)

    def product(kernel, c, lo, width):
        lhs = jnp.concatenate(
            [cat[c, pl.ds(a, rows)].reshape(pixels, 3 * half) for a in range(3)], axis=-1)
        rhs = kernel[:, pl.ds(c * half, half), pl.ds(lo, width)].reshape(9 * half, width)
        return jnp.dot(lhs, rhs, preferred_element_type=jnp.float32)

    def store_half(ref, m, n, first, value):
        for i in range(hq):
            part = value[:, i * LANES:(i + 1) * LANES].reshape(rows, cols, LANES)
            ref[m, n * hq + i, pl.ds(first, rows)] = part.astype(ref.dtype)

    def forward(m):
        for c in range(2):
            @pl.when(stage > 0)
            def _():
                x_main(m, c).wait_recv()

            x_edge(m, c).wait_recv()
            spread(load_half(xin, m, c), c)
            if c == 0:
                acc[...] = product(w, 0, 0, chans)
        for n in range(2):
            z = acc[:, pl.ds(n * half, half)] + product(w, 1, n * half, half)
            sig = jax.nn.sigmoid(z)
            own = load_half(xin, m, n)[1:rows + 1].reshape(pixels, half)
            store_half(xout, m, n, 0, own + z * sig)

            @pl.when(stage < last)
            def _():
                x_edge(m, n).start()
                x_main(m, n).start()

            store_half(slope, m, n, 1, sig * (1.0 + z * (1.0 - sig)))
        slope_edge(m).start()
        for j in range(3):
            x_slice(m, j).start()
        xs[m, me] = xin[m, me, pl.ds(1, rows)]

    def backward(m):
        slope_edge(m).wait_recv()
        for c in range(2):
            @pl.when(stage < last)
            def _():
                g_main(m, c).wait_recv()

            g_edge(m, c).wait_recv()

            d = (load_half(gin, m, c) * load_half(slope, m, c)).astype(dall.dtype)
            for i in range(hq):
                dall[m, me, c * hq + i] = d[1:rows + 1, :, i * LANES:(i + 1) * LANES].reshape(
                    pixels, LANES)
            @pl.when(stage > 0)
            def _():
                spread(d.astype(jnp.float32), c)
                if c == 0:
                    acc[...] = product(wt, 0, 0, chans)

            @pl.when(stage == 0)
            def _():
                d_block(m, c, 1).start()
                d_block(m, c, 0).start()

        @pl.when(stage > 0)
        def _():
            for n in range(2):
                own = load_half(gin, m, n)[1:rows + 1].reshape(pixels, half)
                flow = acc[:, pl.ds(n * half, half)] + product(wt, 1, n * half, half)
                store_half(gout, m, n, 0, own + flow)
                g_edge(m, n).start()
                g_main(m, n).start()
            for c in range(2):
                d_block(m, c, 1).start()
                d_block(m, c, 0).start()

        @pl.when(m > 0)
        def _():
            pass_on(m - 1)

    def prepare(m):
        for j in range(3):
            x_slice(m, j).wait_recv()
        for image in range(2):
            tall = jnp.concatenate([xs[m, image], xs[m, 2 + image]], axis=0).astype(jnp.float32)
            blank_row = jnp.zeros((1, cols, LANES), jnp.float32)
            shifted = column_shifts(tall.reshape(2 * pixels, LANES))
            for b in range(3):
                field = jnp.concatenate(
                    [blank_row, shifted[b].reshape(2 * rows, cols, LANES), blank_row], axis=0)
                for part in range(2):
                    for a in range(3):
                        lo = part * rows + a
                        block = field[lo:lo + rows].reshape(pixels, LANES)
                        xt[m, part, 3 * a + b, :, pl.ds(image * LANES, LANES)] = block.T.astype(
                            xt.dtype)

    def add_grad(m, part):
        blocks = []
        for image in range(2):
            blocks.append(jnp.concatenate(
                [dall[m, part * 2 + image, q] for q in range(quarters)], axis=-1))
        rhs = jnp.concatenate(blocks, axis=0)
        for a in range(3):
            lhs = xt[m, part, pl.ds(3 * a, 3)].reshape(3 * LANES, 2 * pixels)
            total = jnp.dot(lhs, rhs, preferred_element_type=jnp.float32)
            grad[pl.ds(3 * a, 3)] += total.reshape(3, LANES, chans)

    def pass_on(m):
        for c in range(2):
            d_block(m, c, 1).wait_recv()
            d_block(m, c, 2).start()

    def accumulate(m):
        @pl.when(m == micros - 1)
        def _():
            pass_on(m)

        for c in range(2):
            d_block(m, c, 0).wait_recv()
        add_grad(m, sp)
        for c in range(2):
            d_block(m, c, 2).wait_recv()
        add_grad(m, osp)

    F, B, Q, W = ([k * micros + i for i in range(micros)] for k in range(4))
    early = F + Q + [B[0]]
    for i in range(1, micros):
        early += [B[i], W[i - 1]]
    early += [W[-1]]
    late = F + B + Q + W
    final = [F[0]] + [v for pair in zip(F[1:], B) for v in pair] + [B[-1]] + Q + W

    @pl.loop(0, 4 * micros)
    def _(step):
        code = jnp.int32(0)
        for i in range(4 * micros):
            choice = jnp.where(
                stage == last, final[i], jnp.where(stage * 2 < last + 1, early[i], late[i]))
            code = jnp.where(step == i, choice, code)
        kind = code // micros
        m = code % micros

        @pl.when(kind == 0)
        def _():
            forward(m)

        @pl.when(kind == 1)
        def _():
            backward(m)

        @pl.when(kind == 2)
        def _():
            prepare(m)

        @pl.when(kind == 3)
        def _():
            accumulate(m)

    result = pltpu.make_async_copy(grad, out, out_sem)
    result.start()

    @pl.loop(0, micros)
    def _(m):
        slope_edge(m).wait_send()
        for j in range(3):
            x_slice(m, j).wait_send()
        for c in range(2):
            for j in range(3):
                d_block(m, c, j).wait_send()

            @pl.when(stage < last)
            def _():
                x_main(m, c).wait_send()
                x_edge(m, c).wait_send()

            @pl.when(stage == 0)
            def _():
                x_first(m, c).wait_send()

            @pl.when(stage > 0)
            def _():
                g_main(m, c).wait_send()
                g_edge(m, c).wait_send()

            @pl.when(stage == last)
            def _():
                g_first(m, c).wait_send()

    result.wait()


def kernel_shards(images, cotangent, weights):
    micros, imgs, rows, cols, chans = images.shape
    quarters = chans // LANES
    pixels = rows * cols
    bf16, f32 = jnp.bfloat16, jnp.float32
    dma = pltpu.SemaphoreType.DMA
    padded = (micros, quarters, rows + 2, cols, LANES)
    plain = (micros, quarters, rows, cols, LANES)
    flops = 2 * 3 * micros * pixels * 9 * chans * chans
    grads = pl.pallas_call(
        pipeline_kernel,
        out_shape=jax.ShapeDtypeStruct((9, LANES, chans), f32),
        in_specs=[pl.BlockSpec(memory_space=pltpu.HBM)] * 3,
        out_specs=pl.BlockSpec(memory_space=pl.ANY),
        scratch_shapes=[
            pltpu.VMEM((9, chans, chans), bf16),
            pltpu.VMEM((9, chans, chans), bf16),
            pltpu.VMEM(padded, bf16),
            pltpu.VMEM(plain, bf16),
            pltpu.VMEM(padded, bf16),
            pltpu.VMEM(plain, bf16),
            pltpu.VMEM(padded, f32),
            pltpu.VMEM((micros, 4, quarters, pixels, LANES), bf16),
            pltpu.VMEM((micros, 4, rows, cols, LANES), bf16),
            pltpu.VMEM((micros, 2, 9, LANES, 2 * pixels), bf16),
            pltpu.VMEM((pixels, chans), f32),
            pltpu.VMEM((2, rows + 2, cols, 3 * chans // 2), bf16),
            pltpu.VMEM((9, LANES, chans), f32),
            dma, dma((micros, quarters)), dma,
            dma((micros, 2)),
            dma((micros, 2)), dma((micros, 2)), dma((micros, 2)), dma((micros, 2)),
            dma((micros, 2)), dma((micros, 2)), dma((micros, 2)), dma((micros, 2)),
            dma((micros,)), dma((micros,)), dma((micros, 3)), dma((micros, 3)),
            dma((micros, 3, 2)), dma((micros, 3, 2)),
        ],
        compiler_params=pltpu.CompilerParams(
            collective_id=0, has_side_effects=True, vmem_limit_bytes=48 * 2**20),
        cost_estimate=pl.CostEstimate(
            flops=flops, bytes_accessed=2 * 9 * chans * chans * 2, transcendentals=0),
    )(
        images.reshape(micros, rows, cols, chans),
        cotangent.reshape(micros, rows, cols, chans),
        weights.reshape(9, chans, chans),
    )
    return grads[None]


def solution(mesh):
    placed = (
        P(None, "dp", "spatial", None, None),
        P(None, "dp", "spatial", None, None),
        P("chain", None, None, None),
    )

    def program(images, cotangent, weights):
        group = mesh.shape["spatial"] * mesh.shape["dp"]
        fits = (
            mesh.shape["spatial"] == 2
            and mesh.shape["dp"] == 2
            and images.shape[1] == 2
            and weights.shape[2] == group * LANES
            and images.shape[2] * images.shape[3] == 2 * LANES
        )
        return jax.shard_map(
            kernel_shards if fits else shards,
            mesh=mesh,
            in_specs=placed,
            out_specs=P("chain", None, ("spatial", "dp"), None),
            check_vma=False,
        )(images, cotangent, weights)

    return program
```

```python
import jax
import jax.numpy as jnp
from jax import lax
from jax.experimental import pallas as pl
from jax.experimental.pallas import tpu as pltpu
from jax.sharding import PartitionSpec as P


def with_halo(cells, sides, width):
    for axis, dim in sides:
        count = lax.axis_size(axis)
        ends = count - 1
        head = lax.slice_in_dim(cells, 0, width, axis=dim)
        tail = lax.slice_in_dim(cells, cells.shape[dim] - width, cells.shape[dim], axis=dim)
        cells = jnp.concatenate(
            [
                lax.ppermute(tail, axis, [(i, (i + 1) % count) for i in range(ends)]),
                cells,
                lax.ppermute(head, axis, [((i + 1) % count, i) for i in range(ends)]),
            ],
            axis=dim,
        )
    return cells


def passed_along(block, axis, distance):
    devices = range(lax.axis_size(axis))
    route = [(i - distance, i) for i in devices if i - distance in devices]
    return lax.ppermute(block, axis, route)


def patches(padded, rows, cols, reverse):
    offsets = [(a, b) for a in range(3) for b in range(3)]
    if reverse:
        offsets = offsets[::-1]
    parts = [padded[:, a : a + rows, b : b + cols, :] for a, b in offsets]
    return jnp.stack(parts, axis=-2).reshape(-1, 9, padded.shape[-1])


def pad_cols(field):
    return jnp.pad(field, ((0, 0), (0, 0), (1, 1), (0, 0)))


def silu_slope(value):
    sig = jax.nn.sigmoid(value)
    return sig * (1.0 + value * (1.0 - sig))


def shards(images, cotangent, weights):
    micros, imgs, height, width, chans = images.shape
    pixels = imgs * height * width
    sections = lax.axis_size("chain")
    section = lax.axis_index("chain")
    ticks = micros + sections - 1
    kernel = weights[0]
    flat_kernel = kernel.reshape(9 * chans, chans)
    shape_one = (imgs, height, width, chans)

    def forward_tick(tick, carry):
        inbox, saved_x, saved_z = carry
        micro = tick - section
        valid = jnp.logical_and(micro >= 0, micro < micros)
        slot = jnp.clip(micro, 0, micros - 1)
        first = lax.dynamic_index_in_dim(images, slot, 0, keepdims=False)
        source = jnp.where(section == 0, first, inbox)
        rows = with_halo(source, (("spatial", 1),), 1)
        padded = pad_cols(rows)

        def forward_active(operand):
            cols = patches(operand, height, width, False).reshape(-1, 9 * chans)
            state = jnp.dot(cols, flat_kernel, preferred_element_type=jnp.float32)
            output = (source.astype(jnp.float32) + jax.nn.silu(state).reshape(shape_one)).astype(
                jnp.bfloat16
            )
            return (output, state)

        def forward_resting(operand):
            return (jnp.zeros(shape_one, jnp.bfloat16), jnp.zeros((pixels, chans), jnp.float32))

        output, state = lax.cond(valid, forward_active, forward_resting, padded)
        saved_x = jnp.where(
            valid, lax.dynamic_update_index_in_dim(saved_x, padded, slot, 0), saved_x
        )
        saved_z = jnp.where(
            valid, lax.dynamic_update_index_in_dim(saved_z, state, slot, 0), saved_z
        )
        inbox = passed_along(output, "chain", 1)
        return (inbox, saved_x, saved_z)

    start = (
        jnp.zeros(shape_one, jnp.bfloat16),
        jnp.zeros((micros, imgs, height + 2, width + 2, chans), jnp.bfloat16),
        jnp.zeros((micros, pixels, chans), jnp.float32),
    )
    inbox, saved_x, saved_z = lax.fori_loop(0, ticks, forward_tick, start)

    def backward_tick(tick, carry):
        inbox, saved_d = carry
        micro = tick - (sections - 1 - section)
        valid = jnp.logical_and(micro >= 0, micro < micros)
        slot = jnp.clip(micro, 0, micros - 1)
        last = lax.dynamic_index_in_dim(cotangent, slot, 0, keepdims=False)
        upstream = jnp.where(section == sections - 1, last, inbox)
        state = lax.dynamic_index_in_dim(saved_z, slot, 0, keepdims=False)
        delta = (upstream.astype(jnp.float32).reshape(pixels, chans) * silu_slope(state)).astype(
            jnp.bfloat16
        )
        delta = jnp.where(valid, delta, jnp.zeros_like(delta))
        rows = with_halo(delta.reshape(shape_one), (("spatial", 1),), 1)
        padded = pad_cols(rows)

        def backward_active(operand):
            back = patches(operand, height, width, True)
            flow = jnp.einsum("nkc,kdc->nd", back, kernel, preferred_element_type=jnp.float32)
            return (upstream.astype(jnp.float32) + flow.reshape(shape_one)).astype(jnp.bfloat16)

        def backward_resting(operand):
            return jnp.zeros(shape_one, jnp.bfloat16)

        result = lax.cond(valid, backward_active, backward_resting, padded)
        saved_d = jnp.where(
            valid, lax.dynamic_update_index_in_dim(saved_d, delta, slot, 0), saved_d
        )
        inbox = passed_along(result, "chain", -1)
        return (inbox, saved_d)

    begin = (jnp.zeros(shape_one, jnp.bfloat16), jnp.zeros((micros, pixels, chans), jnp.bfloat16))
    inbox, saved_d = lax.fori_loop(0, ticks, backward_tick, begin)
    cols_all = patches(
        saved_x.reshape(micros * imgs, height + 2, width + 2, chans), height, width, False
    )
    cols_all = cols_all.reshape(-1, 9 * chans)
    local_grad = lax.dot_general(
        cols_all,
        saved_d.reshape(-1, chans),
        (((0,), (0,)), ((), ())),
        preferred_element_type=jnp.float32,
    ).reshape(9, chans, chans)
    summed = lax.psum_scatter(
        local_grad.astype(jnp.bfloat16), ("spatial", "dp"), scatter_dimension=1, tiled=True
    ).astype(jnp.float32)
    return summed[None]

LANES = 128
MESH = pl.DeviceIdType.MESH


def pipeline_kernel(
    images, cotangent, weights, out,
    w, wt, first, xin, xout, gin, gout, slope, dall, xs, xt, acc, cat, grad,
    w_sem, loc_sem, out_sem,
    f_send, fm_send, x_send, x_recv, xh_send, xh_recv,
    g_send, g_recv, gh_send, gh_recv,
    s_send, s_recv, xs_send, xs_recv, d_send, d_recv,
):
    micros, quarters, padded_rows, cols, _ = xin.shape
    rows = padded_rows - 2
    pixels = rows * cols
    chans = quarters * LANES
    half = chans // 2
    hq = quarters // 2
    stage = lax.axis_index("chain")
    last = lax.axis_size("chain") - 1
    sp = lax.axis_index("spatial")
    dp = lax.axis_index("dp")
    osp, odp = 1 - sp, 1 - dp
    me = sp * 2 + dp
    mates = ((sp, odp), (osp, dp), (osp, odp))
    edge_src = (rows - 1) * odp
    edge_dst = (rows + 1) * dp
    moved = sp != dp

    def remote(src, dst, send, recv, chain, spatial, core):
        return pltpu.make_async_remote_copy(
            src_ref=src, dst_ref=dst, send_sem=send, recv_sem=recv,
            device_id=(chain, spatial, core), device_id_type=MESH,
        )

    def x_main(m, c):
        return remote(
            xout.at[m, pl.ds(c * hq, hq)], xin.at[m, pl.ds(c * hq, hq), pl.ds(1, rows)],
            x_send.at[m, c], x_recv.at[m, c], stage + 1, sp, dp)

    def x_edge(m, c):
        return remote(
            xout.at[m, pl.ds(c * hq, hq), pl.ds(edge_src, 1)],
            xin.at[m, pl.ds(c * hq, hq), pl.ds(edge_dst, 1)],
            xh_send.at[m, c], xh_recv.at[m, c], stage + 1, sp, odp)

    def first_main(buffer, recv, m, c):
        return remote(
            first.at[m, pl.ds(c * hq, hq)], buffer.at[m, pl.ds(c * hq, hq), pl.ds(1, rows)],
            fm_send.at[m, c], recv.at[m, c], stage, dp, sp)

    def first_edge(buffer, recv, m, c):
        return remote(
            first.at[m, pl.ds(c * hq, hq), pl.ds((rows - 1) * osp, 1)],
            buffer.at[m, pl.ds(c * hq, hq), pl.ds((rows + 1) * sp, 1)],
            f_send.at[m, c], recv.at[m, c], stage, dp, osp)

    def g_main(m, c):
        return remote(
            gout.at[m, pl.ds(c * hq, hq)], gin.at[m, pl.ds(c * hq, hq), pl.ds(1, rows)],
            g_send.at[m, c], g_recv.at[m, c], stage - 1, sp, dp)

    def g_edge(m, c):
        return remote(
            gout.at[m, pl.ds(c * hq, hq), pl.ds(edge_src, 1)],
            gin.at[m, pl.ds(c * hq, hq), pl.ds(edge_dst, 1)],
            gh_send.at[m, c], gh_recv.at[m, c], stage - 1, sp, odp)

    def slope_edge(m):
        return remote(
            slope.at[m, :, pl.ds(1 + edge_src, 1)], slope.at[m, :, pl.ds(edge_dst, 1)],
            s_send.at[m], s_recv.at[m], stage, sp, odp)

    def x_slice(m, j):
        a, b = mates[j]
        return remote(
            xin.at[m, a * 2 + b, pl.ds(1, rows)], xs.at[m, me],
            xs_send.at[m, j], xs_recv.at[m, j], stage, a, b)

    def d_block(m, c, j):
        a, b = ((sp, odp), (osp, dp), (sp, odp))[j]
        owner = me if j < 2 else osp * 2 + dp
        block = dall.at[m, owner, pl.ds(c * hq, hq)]
        return remote(block, block, d_send.at[m, j, c], d_recv.at[m, j, c], stage, a, b)

    def local_in(array, m, q):
        return pltpu.make_async_copy(
            array.at[m, :, :, pl.ds(q * LANES, LANES)], first.at[m, q], loc_sem.at[m, q])

    def hand_out(array, buffer, recv, edge_recv):
        for m in range(micros):
            for q in range(quarters):
                local_in(array, m, q).wait()

            @pl.when(moved)
            def _():
                for c in range(2):
                    first_main(buffer, recv, m, c).start()

            for c in range(2):
                first_edge(buffer, edge_recv, m, c).start()

            @pl.when(jnp.logical_not(moved))
            def _():
                buffer[m, :, pl.ds(1, rows)] = first[m]

    w_copy = pltpu.make_async_copy(weights, w, w_sem)
    w_copy.start()

    @pl.when(stage == 0)
    def _():
        for m in range(micros):
            for q in range(quarters):
                local_in(images, m, q).start()

    @pl.when(stage == last)
    def _():
        for m in range(micros):
            for q in range(quarters):
                local_in(cotangent, m, q).start()

    barrier = pltpu.get_barrier_semaphore()

    def greet(chain, spatial, core):
        pl.semaphore_signal(barrier, inc=1, device_id=(chain, spatial, core), device_id_type=MESH)

    for a, b in mates:
        greet(stage, a, b)

    @pl.when(stage > 0)
    def _():
        greet(stage - 1, sp, dp)
        greet(stage - 1, sp, odp)

    @pl.when(stage < last)
    def _():
        greet(stage + 1, sp, dp)
        greet(stage + 1, sp, odp)

    zero_row = (rows + 1) * dp
    blank = jnp.zeros((micros, quarters, 1, cols, LANES), jnp.float32)
    xin[:, :, pl.ds(zero_row, 1)] = blank.astype(xin.dtype)
    gin[:, :, pl.ds(zero_row, 1)] = blank.astype(gin.dtype)
    slope[:, :, pl.ds(zero_row, 1)] = blank
    grad[...] = jnp.zeros_like(grad)

    around = jnp.where(stage > 0, 2, 0) + jnp.where(stage < last, 2, 0)
    pl.semaphore_wait(barrier, 3 + around)

    @pl.when(stage == 0)
    def _():
        hand_out(images, xin, x_recv, xh_recv)

    @pl.when(stage == last)
    def _():
        hand_out(cotangent, gin, g_recv, gh_recv)

    w_copy.wait()

    @pl.when(stage > 0)
    def _():
        @pl.loop(0, 9)
        def _(k):
            wt[k] = w[8 - k].T

    def column_shifts(value):
        n = value.shape[0]
        col = lax.broadcasted_iota(jnp.int32, value.shape, 0) % cols
        before = jnp.where(col == 0, 0.0, pltpu.roll(value, 1, 0))
        after = jnp.where(col == cols - 1, 0.0, pltpu.roll(value, n - 1, 0))
        return before, value, after

    def load_half(ref, m, c):
        parts = [ref[m, c * hq + i].astype(jnp.float32) for i in range(hq)]
        return jnp.concatenate(parts, axis=-1)

    def spread(value, c):
        shifted = column_shifts(value.reshape(padded_rows * cols, half))
        joined = jnp.concatenate([v.astype(cat.dtype) for v in shifted], axis=-1)
        cat[c] = joined.reshape(padded_rows, cols, 3 * half)

    def product(kernel, c, lo, width):
        lhs = jnp.concatenate(
            [cat[c, pl.ds(a, rows)].reshape(pixels, 3 * half) for a in range(3)], axis=-1)
        rhs = kernel[:, pl.ds(c * half, half), pl.ds(lo, width)].reshape(9 * half, width)
        return jnp.dot(lhs, rhs, preferred_element_type=jnp.float32)

    def store_half(ref, m, n, first, value):
        for i in range(hq):
            part = value[:, i * LANES:(i + 1) * LANES].reshape(rows, cols, LANES)
            ref[m, n * hq + i, pl.ds(first, rows)] = part.astype(ref.dtype)

    def forward(m):
        for c in range(2):
            @pl.when(jnp.logical_or(stage > 0, moved))
            def _():
                x_main(m, c).wait_recv()

            x_edge(m, c).wait_recv()
            spread(load_half(xin, m, c), c)
            if c == 0:
                acc[...] = product(w, 0, 0, chans)
        for n in range(2):
            z = acc[:, pl.ds(n * half, half)] + product(w, 1, n * half, half)
            sig = jax.nn.sigmoid(z)
            own = load_half(xin, m, n)[1:rows + 1].reshape(pixels, half)
            store_half(xout, m, n, 0, own + z * sig)

            @pl.when(stage < last)
            def _():
                x_edge(m, n).start()
                x_main(m, n).start()

            store_half(slope, m, n, 1, sig * (1.0 + z * (1.0 - sig)))
        slope_edge(m).start()
        for j in range(3):
            x_slice(m, j).start()
        xs[m, me] = xin[m, me, pl.ds(1, rows)]

    def backward(m):
        slope_edge(m).wait_recv()
        for c in range(2):
            @pl.when(jnp.logical_or(stage < last, moved))
            def _():
                g_main(m, c).wait_recv()

            g_edge(m, c).wait_recv()

            d = (load_half(gin, m, c) * load_half(slope, m, c)).astype(dall.dtype)
            for i in range(hq):
                dall[m, me, c * hq + i] = d[1:rows + 1, :, i * LANES:(i + 1) * LANES].reshape(
                    pixels, LANES)
            @pl.when(stage > 0)
            def _():
                spread(d.astype(jnp.float32), c)
                if c == 0:
                    acc[...] = product(wt, 0, 0, chans)

            d_block(m, c, 1).start()
            d_block(m, c, 0).start()

        @pl.when(stage > 0)
        def _():
            for n in range(2):
                own = load_half(gin, m, n)[1:rows + 1].reshape(pixels, half)
                flow = acc[:, pl.ds(n * half, half)] + product(wt, 1, n * half, half)
                store_half(gout, m, n, 0, own + flow)
                g_edge(m, n).start()
                g_main(m, n).start()

        @pl.when(m > 0)
        def _():
            pass_on(m - 1)

    def prepare(m):
        for j in range(3):
            x_slice(m, j).wait_recv()
        for image in range(2):
            tall = jnp.concatenate([xs[m, 2 * image], xs[m, 2 * image + 1]], axis=0).astype(jnp.float32)
            blank_row = jnp.zeros((1, cols, LANES), jnp.float32)
            shifted = column_shifts(tall.reshape(2 * pixels, LANES))
            for b in range(3):
                field = jnp.concatenate(
                    [blank_row, shifted[b].reshape(2 * rows, cols, LANES), blank_row], axis=0)
                for part in range(2):
                    for a in range(3):
                        lo = part * rows + a
                        block = field[lo:lo + rows].reshape(pixels, LANES)
                        xt[m, image, 3 * a + b, :, pl.ds(part * LANES, LANES)] = block.T.astype(
                            xt.dtype)

    def add_grad(m, image):
        blocks = []
        for part in range(2):
            blocks.append(jnp.concatenate(
                [dall[m, image * 2 + part, q] for q in range(quarters)], axis=-1))
        rhs = jnp.concatenate(blocks, axis=0)
        for a in range(3):
            lhs = xt[m, image, pl.ds(3 * a, 3)].reshape(3 * LANES, 2 * pixels)
            total = jnp.dot(lhs, rhs, preferred_element_type=jnp.float32)
            grad[pl.ds(3 * a, 3)] += total.reshape(3, LANES, chans)

    def pass_on(m):
        for c in range(2):
            d_block(m, c, 1).wait_recv()
            d_block(m, c, 2).start()

    def accumulate(m):
        @pl.when(m == micros - 1)
        def _():
            pass_on(m)

        for c in range(2):
            d_block(m, c, 0).wait_recv()
        add_grad(m, sp)
        for c in range(2):
            d_block(m, c, 2).wait_recv()
        add_grad(m, osp)

    F, B, Q, W = ([k * micros + i for i in range(micros)] for k in range(4))
    early = F + Q + [B[0]]
    for i in range(1, micros):
        early += [B[i], W[i - 1]]
    early += [W[-1]]
    late = F + B + Q + W
    final = [v for pair in zip(F, B) for v in pair] + Q + W

    @pl.loop(0, 4 * micros)
    def _(step):
        code = jnp.int32(0)
        for i in range(4 * micros):
            choice = jnp.where(
                stage == last, final[i], jnp.where(stage * 2 < last + 1, early[i], late[i]))
            code = jnp.where(step == i, choice, code)
        kind = code // micros
        m = code % micros

        @pl.when(kind == 0)
        def _():
            forward(m)

        @pl.when(kind == 1)
        def _():
            backward(m)

        @pl.when(kind == 2)
        def _():
            prepare(m)

        @pl.when(kind == 3)
        def _():
            accumulate(m)

    result = pltpu.make_async_copy(grad, out, out_sem)
    result.start()

    @pl.loop(0, micros)
    def _(m):
        slope_edge(m).wait_send()
        for j in range(3):
            x_slice(m, j).wait_send()
        for c in range(2):
            for j in range(3):
                d_block(m, c, j).wait_send()

            @pl.when(stage < last)
            def _():
                x_main(m, c).wait_send()
                x_edge(m, c).wait_send()

            @pl.when(stage > 0)
            def _():
                g_main(m, c).wait_send()
                g_edge(m, c).wait_send()

            @pl.when(jnp.logical_or(stage == 0, stage == last))
            def _():
                first_edge(xin, xh_recv, m, c).wait_send()

                @pl.when(moved)
                def _():
                    first_main(xin, x_recv, m, c).wait_send()

    result.wait()


def kernel_shards(images, cotangent, weights):
    micros, imgs, rows, cols, chans = images.shape
    quarters = chans // LANES
    pixels = rows * cols
    bf16, f32 = jnp.bfloat16, jnp.float32
    dma = pltpu.SemaphoreType.DMA
    padded = (micros, quarters, rows + 2, cols, LANES)
    plain = (micros, quarters, rows, cols, LANES)
    flops = 2 * 3 * micros * pixels * 9 * chans * chans
    grads = pl.pallas_call(
        pipeline_kernel,
        out_shape=jax.ShapeDtypeStruct((9, LANES, chans), f32),
        in_specs=[pl.BlockSpec(memory_space=pltpu.HBM)] * 3,
        out_specs=pl.BlockSpec(memory_space=pl.ANY),
        scratch_shapes=[
            pltpu.VMEM((9, chans, chans), bf16),
            pltpu.VMEM((9, chans, chans), bf16),
            pltpu.VMEM(plain, bf16),
            pltpu.VMEM(padded, bf16),
            pltpu.VMEM(plain, bf16),
            pltpu.VMEM(padded, bf16),
            pltpu.VMEM(plain, bf16),
            pltpu.VMEM(padded, f32),
            pltpu.VMEM((micros, 4, quarters, pixels, LANES), bf16),
            pltpu.VMEM((micros, 4, rows, cols, LANES), bf16),
            pltpu.VMEM((micros, 2, 9, LANES, 2 * pixels), bf16),
            pltpu.VMEM((pixels, chans), f32),
            pltpu.VMEM((2, rows + 2, cols, 3 * chans // 2), bf16),
            pltpu.VMEM((9, LANES, chans), f32),
            dma, dma((micros, quarters)), dma,
            dma((micros, 2)), dma((micros, 2)),
            dma((micros, 2)), dma((micros, 2)), dma((micros, 2)), dma((micros, 2)),
            dma((micros, 2)), dma((micros, 2)), dma((micros, 2)), dma((micros, 2)),
            dma((micros,)), dma((micros,)), dma((micros, 3)), dma((micros, 3)),
            dma((micros, 3, 2)), dma((micros, 3, 2)),
        ],
        compiler_params=pltpu.CompilerParams(
            collective_id=0, has_side_effects=True, vmem_limit_bytes=48 * 2**20),
        cost_estimate=pl.CostEstimate(
            flops=flops, bytes_accessed=2 * 9 * chans * chans * 2, transcendentals=0),
    )(
        images.reshape(micros, rows, cols, chans),
        cotangent.reshape(micros, rows, cols, chans),
        weights.reshape(9, chans, chans),
    )
    return grads[None]


def solution(mesh):
    placed = (
        P(None, "dp", "spatial", None, None),
        P(None, "dp", "spatial", None, None),
        P("chain", None, None, None),
    )

    def program(images, cotangent, weights):
        group = mesh.shape["spatial"] * mesh.shape["dp"]
        fits = (
            mesh.shape["spatial"] == 2
            and mesh.shape["dp"] == 2
            and images.shape[1] == 2
            and weights.shape[2] == group * LANES
            and images.shape[2] * images.shape[3] == 2 * LANES
        )
        return jax.shard_map(
            kernel_shards if fits else shards,
            mesh=mesh,
            in_specs=placed,
            out_specs=P("chain", None, ("spatial", "dp"), None),
            check_vma=False,
        )(images, cotangent, weights)

    return program
```
